32 devices in a mesh: tm: 4 (over y, core), slab: 8 (over z, x).
Axes of the slice: x: 2, y: 2, z: 4, core: 2. Of those that a mesh axis runs over, the one named last changes fastest.
Arguments:
- solutions: float32 [4, 96, 8192], P('tm', None, 'slab'), may hold values from -6 to 6
- eigvecs: float32 [4, 2, 192, 3, 8192], P('tm', None, None, None, 'slab'), may hold values from -0.02734375 to 0.02734375
- sink_noise: int32 [192, 4, 4], P(None, 'tm'), may hold values from 0 to 3
- eig_block: int32 [192], replicated, may hold values from 0 to 7
Outputs:
- projected: float32 [192, 4, 2, 16], P('slab', 'tm')
- sink_line: float32 [2, 8, 4], replicated
The draws below stay inside these ranges and needn't reach their ends.
All inputs are finite; a program needn't handle non-finite values.
Results may differ from the reference program's by a relative error of at most 0.000092.
Values sent between devices are 32-bit elements; how exact they have to be, the bound alone decides.
No kernel may reach another device: no remote copies, remote signals or barrier semaphores. Data moves between devices by JAX's collectives and lax.ppermute only.
A program may use at most 128 MiB of HBM per device.

```python
import math
import jax
import jax.numpy as jnp
from jax import lax

NSPIN = 4
NCOLOR = 3
NEIG = 192
NBLOCK = 8
BLX = 8
BLY = 16
ZM = 1
NT = 4
SITES = 8192
N_SLAB = 8


def set_ends(array, rng, least, top_value):
    spot = [jax.random.randint(jax.random.fold_in(rng, axis), (), 0, length) for axis, length in enumerate(array.shape)]
    widest = array.shape.index(max(array.shape))
    neighbour = spot[:widest] + [(spot[widest] + 1) % array.shape[widest]] + spot[widest + 1:]
    return array.at[tuple(spot)].set(least).at[tuple(neighbour)].set(top_value)


def shard_levels(key, shape, shards, low, high):
    factor_of, own = 1.0, jax.random.fold_in(key, 6)
    for dim, blocks in shards:
        heights = jnp.exp(jax.random.uniform(jax.random.fold_in(own, dim), (blocks,), jnp.float32, low / len(shards), high / len(shards)))
        factor_of = factor_of * jnp.repeat(heights, shape[dim] // blocks).reshape([-1 if axis == dim else 1 for axis in range(len(shape))])
    return factor_of


def noise(key, extent, deviation, limit, pieces=(), kind=jnp.bfloat16):
    gain = shard_levels(key, extent, pieces, -0.22, 0.18) if pieces else 1.0
    array = jax.random.normal(key, extent, jnp.float32) * deviation * gain
    return jnp.minimum(jnp.maximum(array, -limit), limit).astype(kind)


def setup_inputs(seed: int = 0) -> dict:
    splits = jax.random.split(jax.random.key(seed), 5)
    solutions = noise(splits[0], (NT, 2 * NSPIN * NSPIN * NCOLOR, SITES), 1.0, 6.0, ((0, 4), (2, 8)), jnp.float32)
    eigvecs = noise(splits[1], (NT, 2, NEIG, NCOLOR, SITES), (2 * NCOLOR * SITES) ** -0.5, 0.02734375, ((0, 4), (4, 8)), jnp.float32)
    sink_noise = set_ends(jax.random.randint(splits[2], (NEIG, NT, NSPIN), 0, 4), jax.random.fold_in(splits[2], 1), 0, 3).astype(jnp.int32)
    eig_block = set_ends(jax.random.randint(splits[3], (NEIG,), 0, NBLOCK), jax.random.fold_in(splits[3], 1), 0, NBLOCK - 1).astype(jnp.int32)
    return {"solutions": solutions, "eigvecs": eigvecs, "sink_noise": sink_noise, "eig_block": eig_block}


def project(vectors, columns):
    product = jnp.einsum('akcs,bjcs->abkj', vectors, columns, precision=lax.Precision.HIGHEST)
    return jnp.stack((product[0, 0] + product[1, 1], product[0, 1] - product[1, 0]), axis=1)

def line_part(parts, sink_noise, eig_block):
    real_part = parts[:, :, 0]
    imag_part = parts[:, :, 1]
    zreal = ((sink_noise == 0).astype(jnp.float32) - (sink_noise == 2).astype(jnp.float32))[..., None]
    zimag = ((sink_noise == 1).astype(jnp.float32) - (sink_noise == 3).astype(jnp.float32))[..., None]
    line_real = lax.optimization_barrier(jnp.sum(zreal * real_part + zimag * imag_part, axis=(1, 2)))
    line_imag = lax.optimization_barrier(jnp.sum(zreal * imag_part - zimag * real_part, axis=(1, 2)))
    onehot = (eig_block[:, None] == jnp.arange(NBLOCK, dtype=jnp.int32)[None, :]).astype(jnp.float32)
    return jnp.stack((jnp.dot(onehot.T, line_real, precision=lax.Precision.HIGHEST), jnp.dot(onehot.T, line_imag, precision=lax.Precision.HIGHEST)))

def reference(solutions, eigvecs, sink_noise, eig_block):
    spin_pairs = NSPIN * NSPIN
    field = solutions.reshape(NT, 2, spin_pairs, NCOLOR, N_SLAB, BLX * BLY * ZM, N_SLAB)
    field = jnp.transpose(field, (0, 1, 2, 3, 6, 5, 4)).reshape(NT, 2, spin_pairs, NCOLOR, -1)
    result = lax.map(lambda operands: project(operands[0], operands[1]), (eigvecs, field))
    projected = jnp.transpose(result, (1, 0, 2, 3))
    parts = projected.reshape(NEIG, NT, 2, NSPIN, NSPIN)
    factor = 1.0 / math.sqrt(NT * NEIG * NSPIN / NBLOCK)
    sink_line = line_part(parts, sink_noise, eig_block) * factor
    return (projected, sink_line)
```

```python
import functools
import math

import jax
import jax.numpy as jnp
from jax import lax
from jax.experimental import pallas as pl
from jax.experimental.pallas import tpu as pltpu
from jax.sharding import PartitionSpec as P

NSPIN = 4
NCOLOR = 3
NEIG = 192
NBLOCK = 8
PAIRS = NSPIN * NSPIN
COLS = 2 * PAIRS
GROUPS = 128 // COLS
LINE_LANE = 96

VMEM = pl.BlockSpec(memory_space=pltpu.VMEM)
SMEM = pl.BlockSpec(memory_space=pltpu.SMEM)


def split(value):
    high = value.astype(jnp.bfloat16)
    low = (value - high.astype(jnp.float32)).astype(jnp.bfloat16)
    return high, low


def pack_kernel(count, sol_ref, out_ref, tiles, turned):
    width = sol_ref.shape[1] // GROUPS
    rows = width // count
    for i in range(tiles.shape[0]):
        tiles[i] = sol_ref[:, pl.ds(128 * i, 128)]
    per_group = width // 128
    for color in range(NCOLOR):
        for i in range(per_group):
            stacked = jnp.concatenate(
                [tiles[g * per_group + i, pl.ds(color, COLS, stride=NCOLOR), :] for g in range(GROUPS)], axis=0
            )
            turned[pl.ds(128 * i, 128), :] = stacked.T
        for r in range(count):
            out_ref[r, pl.ds(color * rows, rows), :] = turned[pl.ds(r, rows, stride=count), :]


def project_kernel(count, field_ref, vec_ref, noise_ref, block_ref, out_ref, weights):
    width = vec_ref.shape[3] // GROUPS
    rows = width // count
    per = NEIG // count
    for color in range(NCOLOR):
        for s in range(count):
            weights[pl.ds(color * width + s, rows, stride=count), :] = field_ref[s, pl.ds(color * rows, rows), :]
    high, low = split(weights[...])
    both = jnp.concatenate([high, low], axis=1)
    lane = lax.broadcasted_iota(jnp.int32, (NEIG, 128), 1)
    sums = []
    for part in range(2):
        total = jnp.zeros((NEIG, 128), jnp.float32)
        for g in range(GROUPS):
            vec = jnp.concatenate([vec_ref[part, color, :, pl.ds(g * width, width)] for color in range(NCOLOR)], axis=1)
            vec_high, vec_low = split(vec)
            first = jnp.dot(vec_high, both, preferred_element_type=jnp.float32)
            second = jnp.dot(vec_low, high, preferred_element_type=jnp.float32)
            value = first[:, :128] + (first[:, 128:] + second)
            total = jnp.where(lane // COLS == g, value, total)
        shift = 64
        while shift >= COLS:
            total = total + pltpu.roll(total, shift, axis=1)
            shift //= 2
        sums.append(total)
    swapped = pltpu.roll(sums[1], PAIRS, axis=1)
    product = sums[0] + jnp.where(lane % COLS < PAIRS, swapped, -swapped)
    turned = product.T[:COLS]
    real, imag = turned[:PAIRS], turned[PAIRS:]
    noise = jnp.concatenate(
        [jnp.broadcast_to(noise_ref[pl.ds(spin, 1), :], (NSPIN, NEIG)) for spin in range(NSPIN)], axis=0
    )
    zreal = (noise == 0).astype(jnp.float32) - (noise == 2).astype(jnp.float32)
    zimag = (noise == 1).astype(jnp.float32) - (noise == 3).astype(jnp.float32)
    line = jnp.concatenate([zreal * real + zimag * imag, zreal * imag - zimag * real], axis=0)
    blocks = lax.broadcasted_iota(jnp.int32, (NBLOCK, NEIG), 0)
    onehot = (blocks == block_ref[...]).astype(jnp.bfloat16)
    line_high, line_low = split(line)
    dims = (((1,), (1,)), ((), ()))
    line_sum = lax.dot_general(onehot, line_high, dims, preferred_element_type=jnp.float32)
    line_sum += lax.dot_general(onehot, line_low, dims, preferred_element_type=jnp.float32)
    packed = [None] * count
    for j in range(count):
        pieces = [turned[8 * i : 8 * i + 8, per * j : per * (j + 1)] for i in range(COLS // 8)]
        used = per * len(pieces)
        if used < LINE_LANE:
            pieces.append(jnp.zeros((8, LINE_LANE - used), jnp.float32))
        packed[j] = jnp.concatenate(pieces + [line_sum], axis=1)
    for i in range(out_ref.shape[0]):
        for j in range(count):
            out_ref[i, j] = packed[j]


def finish_kernel(count, factor, index_ref, parts_ref, rows_ref, line_ref):
    per = NEIG // count
    own = jnp.sum(parts_ref[index_ref[0]], axis=0)
    for i in range(COLS // 8):
        rows_ref[pl.ds(8 * i, 8), :] = own[:, per * i : per * (i + 1)]
    whole = jnp.sum(jnp.sum(parts_ref[...], axis=1), axis=0)
    turned = whole.T[LINE_LANE:]
    for part in range(2):
        first = PAIRS * part
        line_ref[part] = factor * sum(turned[first + NSPIN * s : first + NSPIN * (s + 1)] for s in range(NSPIN))


def body(solutions, eigvecs, sink_noise, eig_block):
    count = lax.axis_size("slab")
    times = lax.axis_size("tm")
    sites = solutions.shape[-1]
    rows = NCOLOR * sites // GROUPS // count
    per = NEIG // count
    f32 = jnp.float32
    chunks = pl.pallas_call(
        functools.partial(pack_kernel, count),
        out_shape=jax.ShapeDtypeStruct((count, rows, 128), f32),
        in_specs=[VMEM],
        out_specs=VMEM,
        scratch_shapes=[pltpu.VMEM((sites // 128, NCOLOR * COLS, 128), f32), pltpu.VMEM((sites // GROUPS, 128), f32)],
        compiler_params=pltpu.CompilerParams(vmem_limit_bytes=8 * 1024 * 1024),
        name="pack",
    )(solutions.reshape(solutions.shape[1:]))
    received = lax.all_to_all(chunks, "slab", split_axis=0, concat_axis=0, tiled=True)
    vectors = jnp.transpose(eigvecs.reshape(eigvecs.shape[1:]), (0, 2, 1, 3))
    parts = pl.pallas_call(
        functools.partial(project_kernel, count),
        out_shape=jax.ShapeDtypeStruct((times, count, 8, 128), f32),
        in_specs=[VMEM] * 4,
        out_specs=VMEM,
        scratch_shapes=[pltpu.VMEM((NCOLOR * sites // GROUPS, 128), f32)],
        compiler_params=pltpu.CompilerParams(vmem_limit_bytes=32 * 1024 * 1024),
        name="project",
    )(received, vectors, jnp.transpose(sink_noise.reshape(NEIG, NSPIN)), eig_block.reshape(1, NEIG))
    parts = lax.all_to_all(parts.reshape(times * count, 8, 128), ("tm", "slab"), split_axis=0, concat_axis=0, tiled=True)
    factor = 1.0 / math.sqrt(times * NEIG * NSPIN / NBLOCK)
    own_rows, line = pl.pallas_call(
        functools.partial(finish_kernel, count, factor),
        out_shape=(jax.ShapeDtypeStruct((COLS, per), f32), jax.ShapeDtypeStruct((2, NSPIN, NBLOCK), f32)),
        in_specs=[SMEM, VMEM],
        out_specs=(VMEM, VMEM),
        compiler_params=pltpu.CompilerParams(vmem_limit_bytes=8 * 1024 * 1024),
        name="finish",
    )(lax.axis_index("tm").reshape(1), parts.reshape(times, count, 8, 128))
    projected = jnp.transpose(own_rows).reshape(per, 1, 2, PAIRS)
    return projected, jnp.transpose(line, (0, 2, 1))


def solution(mesh):
    in_specs = (P("tm", None, "slab"), P("tm", None, None, None, "slab"), P(None, "tm", None), P())
    out_specs = (P("slab", "tm", None, None), P())
    return jax.shard_map(body, mesh=mesh, in_specs=in_specs, out_specs=out_specs, check_vma=False)
```

```python
import functools
import math

import jax
import jax.numpy as jnp
from jax import lax
from jax.experimental import pallas as pl
from jax.experimental.pallas import tpu as pltpu
from jax.sharding import PartitionSpec as P

NSPIN = 4
NCOLOR = 3
NEIG = 192
NBLOCK = 8
PAIRS = NSPIN * NSPIN
COLS = 2 * PAIRS
GROUPS = 128 // COLS
LINE_LANE = 96

ORDER = (4, 6, 5, 7, 1, 3, 2)

VMEM = pl.BlockSpec(memory_space=pltpu.VMEM)
SMEM = pl.BlockSpec(memory_space=pltpu.SMEM)


def split(value):
    high = value.astype(jnp.bfloat16)
    low = (value - high.astype(jnp.float32)).astype(jnp.bfloat16)
    return high, low


def pack_kernel(partners, index_ref, sol_ref, *refs):
    out_refs, (tiles, turned) = refs[: len(partners)], refs[len(partners) :]
    count = len(partners)
    width = sol_ref.shape[1] // GROUPS
    rows = width // count
    per_group = width // 128
    for i in range(tiles.shape[0]):
        tiles[i] = sol_ref[:, pl.ds(128 * i, 128)]
    for color in range(NCOLOR):
        for i in range(per_group):
            stacked = jnp.concatenate(
                [tiles[g * per_group + i, pl.ds(color, COLS, stride=NCOLOR), :] for g in range(GROUPS)], axis=0
            )
            turned[pl.ds(128 * i, 128), :] = stacked.T
        for partner, out_ref in zip(partners, out_refs):
            r = jnp.bitwise_xor(index_ref[0], partner)
            out_ref[pl.ds(color * rows, rows), :] = turned[pl.ds(r, rows, stride=count), :]


def split_kernel(vec_ref, high_ref, low_ref):
    width = vec_ref.shape[3] // GROUPS
    for part in range(2):
        for g in range(GROUPS):
            rows = pl.ds((part * GROUPS + g) * NEIG, NEIG)
            for color in range(NCOLOR):
                lanes = pl.ds(color * width, width)
                high, low = split(vec_ref[part, color, :, pl.ds(g * width, width)])
                high_ref[rows, lanes] = high
                low_ref[rows, lanes] = low


def project_kernel(partners, index_ref, *refs):
    count = len(partners)
    field_refs = refs[:count]
    high_ref, low_ref, noise_ref, block_ref, out_ref, weights = refs[count:]
    width = high_ref.shape[1] // NCOLOR
    rows = width // count
    per = NEIG // count
    for partner, field_ref in zip(partners, field_refs):
        s = jnp.bitwise_xor(index_ref[0], partner)
        for color in range(NCOLOR):
            weights[pl.ds(color * width + s, rows, stride=count), :] = field_ref[pl.ds(color * rows, rows), :]
    high, low = split(weights[...])
    first = jnp.dot(high_ref[...], jnp.concatenate([high, low], axis=1), preferred_element_type=jnp.float32)
    second = jnp.dot(low_ref[...], high, preferred_element_type=jnp.float32)
    products = first[:, :128] + (first[:, 128:] + second)
    lane = lax.broadcasted_iota(jnp.int32, (NEIG, 128), 1)
    sums = []
    for part in range(2):
        total = products[part * GROUPS * NEIG :][:NEIG]
        for g in range(1, GROUPS):
            total = jnp.where(lane // COLS == g, products[(part * GROUPS + g) * NEIG :][:NEIG], total)
        shift = 64
        while shift >= COLS:
            total = total + pltpu.roll(total, shift, axis=1)
            shift //= 2
        sums.append(total)
    swapped = pltpu.roll(sums[1], PAIRS, axis=1)
    product = sums[0] + jnp.where(lane % COLS < PAIRS, swapped, -swapped)
    turned = product.T[:COLS]
    real, imag = turned[:PAIRS], turned[PAIRS:]
    noise = jnp.concatenate(
        [jnp.broadcast_to(noise_ref[pl.ds(spin, 1), :], (NSPIN, NEIG)) for spin in range(NSPIN)], axis=0
    )
    zreal = (noise == 0).astype(jnp.float32) - (noise == 2).astype(jnp.float32)
    zimag = (noise == 1).astype(jnp.float32) - (noise == 3).astype(jnp.float32)
    line = jnp.concatenate([zreal * real + zimag * imag, zreal * imag - zimag * real], axis=0)
    blocks = lax.broadcasted_iota(jnp.int32, (NBLOCK, NEIG), 0)
    onehot = (blocks == block_ref[...]).astype(jnp.bfloat16)
    line_high, line_low = split(line)
    dims = (((1,), (1,)), ((), ()))
    line_sum = lax.dot_general(onehot, line_high, dims, preferred_element_type=jnp.float32)
    line_sum += lax.dot_general(onehot, line_low, dims, preferred_element_type=jnp.float32)
    packed = [None] * count
    for j in range(count):
        pieces = [turned[8 * i : 8 * i + 8, per * j : per * (j + 1)] for i in range(COLS // 8)]
        used = per * len(pieces)
        if used < LINE_LANE:
            pieces.append(jnp.zeros((8, LINE_LANE - used), jnp.float32))
        packed[j] = jnp.concatenate(pieces + [line_sum], axis=1)
    for i in range(out_ref.shape[0]):
        for j in range(count):
            out_ref[i, j] = packed[j]


def finish_kernel(count, factor, index_ref, parts_ref, rows_ref, line_ref):
    per = NEIG // count
    own = jnp.sum(parts_ref[index_ref[0]], axis=0)
    for i in range(COLS // 8):
        rows_ref[pl.ds(8 * i, 8), :] = own[:, per * i : per * (i + 1)]
    whole = jnp.sum(jnp.sum(parts_ref[...], axis=1), axis=0)
    turned = whole.T[LINE_LANE:]
    for part in range(2):
        first = PAIRS * part
        line_ref[part] = factor * sum(turned[first + NSPIN * s : first + NSPIN * (s + 1)] for s in range(NSPIN))


def body(solutions, eigvecs, sink_noise, eig_block):
    count = lax.axis_size("slab")
    times = lax.axis_size("tm")
    sites = solutions.shape[-1]
    rows = NCOLOR * sites // GROUPS // count
    per = NEIG // count
    f32 = jnp.float32
    index = lax.axis_index("slab").reshape(1)
    far = [p for p in ORDER if p < count]
    partners = [0] + far + [p for p in range(1, count) if p not in far]
    chunks = pl.pallas_call(
        functools.partial(pack_kernel, partners),
        out_shape=[jax.ShapeDtypeStruct((rows, 128), f32)] * count,
        in_specs=[SMEM, VMEM],
        out_specs=[VMEM] * count,
        scratch_shapes=[pltpu.VMEM((sites // 128, NCOLOR * COLS, 128), f32), pltpu.VMEM((sites // GROUPS, 128), f32)],
        compiler_params=pltpu.CompilerParams(vmem_limit_bytes=8 * 1024 * 1024),
        name="pack",
    )(index, solutions.reshape(solutions.shape[1:]))
    received = [
        lax.ppermute(chunk, "slab", [(i, i ^ partner) for i in range(count)]) if partner else chunk
        for partner, chunk in zip(partners, chunks)
    ]
    vectors = jnp.transpose(eigvecs.reshape(eigvecs.shape[1:]), (0, 2, 1, 3))
    shape = jax.ShapeDtypeStruct((2 * GROUPS * NEIG, NCOLOR * sites // GROUPS), jnp.bfloat16)
    high, low = pl.pallas_call(
        split_kernel,
        out_shape=(shape, shape),
        in_specs=[VMEM],
        out_specs=(VMEM, VMEM),
        compiler_params=pltpu.CompilerParams(vmem_limit_bytes=24 * 1024 * 1024),
        cost_estimate=pl.CostEstimate(flops=6 * eigvecs.size, bytes_accessed=8 * eigvecs.size, transcendentals=0),
        name="split",
    )(vectors)
    parts = pl.pallas_call(
        functools.partial(project_kernel, partners),
        out_shape=jax.ShapeDtypeStruct((times, count, 8, 128), f32),
        in_specs=[SMEM] + [VMEM] * (count + 4),
        out_specs=VMEM,
        scratch_shapes=[pltpu.VMEM((NCOLOR * sites // GROUPS, 128), f32)],
        compiler_params=pltpu.CompilerParams(vmem_limit_bytes=24 * 1024 * 1024),
        name="project",
    )(index, *received, high, low, jnp.transpose(sink_noise.reshape(NEIG, NSPIN)), eig_block.reshape(1, NEIG))
    parts = lax.all_to_all(parts.reshape(times * count, 8, 128), ("tm", "slab"), split_axis=0, concat_axis=0, tiled=True)
    factor = 1.0 / math.sqrt(times * NEIG * NSPIN / NBLOCK)
    own_rows, line = pl.pallas_call(
        functools.partial(finish_kernel, count, factor),
        out_shape=(jax.ShapeDtypeStruct((COLS, per), f32), jax.ShapeDtypeStruct((2, NSPIN, NBLOCK), f32)),
        in_specs=[SMEM, VMEM],
        out_specs=(VMEM, VMEM),
        compiler_params=pltpu.CompilerParams(vmem_limit_bytes=8 * 1024 * 1024),
        name="finish",
    )(lax.axis_index("tm").reshape(1), parts.reshape(times, count, 8, 128))
    projected = jnp.transpose(own_rows).reshape(per, 1, 2, PAIRS)
    return projected, jnp.transpose(line, (0, 2, 1))


def solution(mesh):
    in_specs = (P("tm", None, "slab"), P("tm", None, None, None, "slab"), P(None, "tm", None), P())
    out_specs = (P("slab", "tm", None, None), P())
    return jax.shard_map(body, mesh=mesh, in_specs=in_specs, out_specs=out_specs, check_vma=False)
```

```python
import functools
import math

import jax
import jax.numpy as jnp
from jax import lax
from jax.experimental import pallas as pl
from jax.experimental.pallas import tpu as pltpu
from jax.sharding import PartitionSpec as P

NSPIN = 4
NCOLOR = 3
NEIG = 192
NBLOCK = 8
PAIRS = NSPIN * NSPIN
COLS = 2 * PAIRS
GROUPS = 128 // COLS
LINE_LANE = 96

ORDER = (4, 6, 5, 7, 1, 3, 2)

VMEM = pl.BlockSpec(memory_space=pltpu.VMEM)
SMEM = pl.BlockSpec(memory_space=pltpu.SMEM)


def split(value):
    high = value.astype(jnp.bfloat16)
    low = (value - high.astype(jnp.float32)).astype(jnp.bfloat16)
    return high, low


def pack_kernel(partners, index_ref, time_ref, sol_ref, *refs):
    out_refs, (tiles, turned) = refs[: len(partners)], refs[len(partners) :]
    count = len(partners)
    width = sol_ref.shape[1] // GROUPS
    rows = width // count
    per_group = width // 128
    for i in range(tiles.shape[0]):
        tiles[i] = sol_ref[:, pl.ds(128 * i, 128)]
    for color in range(NCOLOR):
        for i in range(per_group):
            stacked = jnp.concatenate(
                [tiles[g * per_group + i, pl.ds(color, COLS, stride=NCOLOR), :] for g in range(GROUPS)], axis=0
            )
            turned[pl.ds(128 * i, 128), :] = stacked.T
        for partner, out_ref in zip(partners, out_refs):
            r = jnp.bitwise_xor(index_ref[0], partner)
            out_ref[pl.ds(color * rows, rows), :] = turned[pl.ds(r, rows, stride=count), :]


def split_kernel(vec_ref, high_ref, low_ref, landed, arrived):
    width = vec_ref.shape[3] // GROUPS
    steps = [(part, color) for color in range(NCOLOR) for part in range(2)]
    copies = [
        pltpu.make_async_copy(vec_ref.at[part, color], landed.at[part, color], arrived.at[i])
        for i, (part, color) in enumerate(steps)
    ]
    for copy in copies:
        copy.start()
    for copy, (part, color) in zip(copies, steps):
        copy.wait()
        for g in range(GROUPS):
            rows = pl.ds((g * 2 + part) * NEIG, NEIG)
            lanes = pl.ds(color * width, width)
            high, low = split(landed[part, color, :, pl.ds(g * width, width)])
            high_ref[rows, lanes] = high
            low_ref[rows, lanes] = low


def project_kernel(partners, index_ref, *refs):
    count = len(partners)
    field_refs = refs[:count]
    high_ref, low_ref, noise_ref, block_ref, out_ref, weights = refs[count:]
    width = high_ref.shape[1] // NCOLOR
    rows = width // count
    per = NEIG // count
    for partner, field_ref in zip(partners, field_refs):
        s = jnp.bitwise_xor(index_ref[0], partner)
        for color in range(NCOLOR):
            weights[pl.ds(color * width + s, rows, stride=count), :] = field_ref[pl.ds(color * rows, rows), :]
    high, low = split(weights[...].T)
    dims = (((1,), (1,)), ((), ()))
    total = jnp.zeros((COLS, 2 * NEIG), jnp.float32)
    for g in range(GROUPS):
        vecs, columns = pl.ds(g * 2 * NEIG, 2 * NEIG), slice(g * COLS, (g + 1) * COLS)
        both = jnp.concatenate([high[columns], low[columns]], axis=0)
        first = lax.dot_general(both, high_ref[vecs, :], dims, preferred_element_type=jnp.float32)
        second = lax.dot_general(high[columns], low_ref[vecs, :], dims, preferred_element_type=jnp.float32)
        total += first[:COLS] + (first[COLS:] + second)
    with_real, with_imag = total[:, :NEIG], total[:, NEIG:]
    real = with_real[:PAIRS] + with_imag[PAIRS:]
    imag = with_real[PAIRS:] - with_imag[:PAIRS]
    noise = jnp.concatenate(
        [jnp.broadcast_to(noise_ref[pl.ds(spin, 1), :], (NSPIN, NEIG)) for spin in range(NSPIN)], axis=0
    )
    zreal = (noise == 0).astype(jnp.float32) - (noise == 2).astype(jnp.float32)
    zimag = (noise == 1).astype(jnp.float32) - (noise == 3).astype(jnp.float32)
    line = jnp.concatenate([zreal * real + zimag * imag, zreal * imag - zimag * real], axis=0)
    blocks = lax.broadcasted_iota(jnp.int32, (NBLOCK, NEIG), 0)
    onehot = (blocks == block_ref[...]).astype(jnp.bfloat16)
    line_high, line_low = split(line)
    line_sum = lax.dot_general(onehot, line_high, dims, preferred_element_type=jnp.float32)
    line_sum += lax.dot_general(onehot, line_low, dims, preferred_element_type=jnp.float32)
    sums = jnp.concatenate([real, imag], axis=0)
    packed = [None] * count
    for j in range(count):
        pieces = [sums[8 * i : 8 * i + 8, per * j : per * (j + 1)] for i in range(COLS // 8)]
        used = per * len(pieces)
        if used < LINE_LANE:
            pieces.append(jnp.zeros((8, LINE_LANE - used), jnp.float32))
        packed[j] = jnp.concatenate(pieces + [line_sum], axis=1)
    for i in range(out_ref.shape[0]):
        for j in range(count):
            out_ref[i, j] = packed[j]


def finish_kernel(count, factor, index_ref, parts_ref, rows_ref, line_ref):
    per = NEIG // count
    own = jnp.sum(parts_ref[index_ref[0]], axis=0)
    for i in range(COLS // 8):
        rows_ref[pl.ds(8 * i, 8), :] = own[:, per * i : per * (i + 1)]
    whole = jnp.sum(jnp.sum(parts_ref[...], axis=1), axis=0)
    turned = whole.T[LINE_LANE:]
    for part in range(2):
        first = PAIRS * part
        line_ref[part] = factor * sum(turned[first + NSPIN * s : first + NSPIN * (s + 1)] for s in range(NSPIN))


def body(solutions, eigvecs, sink_noise, eig_block):
    count = lax.axis_size("slab")
    times = lax.axis_size("tm")
    sites = solutions.shape[-1]
    rows = NCOLOR * sites // GROUPS // count
    per = NEIG // count
    f32 = jnp.float32
    index = lax.axis_index("slab").reshape(1)
    time = lax.axis_index("tm").reshape(1)
    far = [p for p in ORDER if p < count]
    partners = [0] + far + [p for p in range(1, count) if p not in far]
    chunks = pl.pallas_call(
        functools.partial(pack_kernel, partners),
        out_shape=[jax.ShapeDtypeStruct((rows, 128), f32)] * count,
        in_specs=[SMEM, SMEM, VMEM],
        out_specs=[VMEM] * count,
        scratch_shapes=[pltpu.VMEM((sites // 128, NCOLOR * COLS, 128), f32), pltpu.VMEM((sites // GROUPS, 128), f32)],
        compiler_params=pltpu.CompilerParams(vmem_limit_bytes=8 * 1024 * 1024),
        name="pack",
    )(index, time, solutions.reshape(solutions.shape[1:]))
    received = [
        lax.ppermute(chunk, "slab", [(i, i ^ partner) for i in range(count)]) if partner else chunk
        for partner, chunk in zip(partners, chunks)
    ]
    vectors = jnp.transpose(eigvecs.reshape(eigvecs.shape[1:]), (0, 2, 1, 3))
    shape = jax.ShapeDtypeStruct((2 * GROUPS * NEIG, NCOLOR * sites // GROUPS), jnp.bfloat16)
    high, low = pl.pallas_call(
        split_kernel,
        out_shape=(shape, shape),
        in_specs=[pl.BlockSpec(memory_space=pltpu.HBM)],
        out_specs=(VMEM, VMEM),
        scratch_shapes=[pltpu.VMEM(vectors.shape, f32), pltpu.SemaphoreType.DMA((2 * NCOLOR,))],
        compiler_params=pltpu.CompilerParams(vmem_limit_bytes=24 * 1024 * 1024),
        cost_estimate=pl.CostEstimate(flops=6 * eigvecs.size, bytes_accessed=8 * eigvecs.size, transcendentals=0),
        name="split",
    )(pltpu.with_memory_space_constraint(vectors, pltpu.HBM))
    parts = pl.pallas_call(
        functools.partial(project_kernel, partners),
        out_shape=pltpu.VMEM((times, count, 8, 128), f32),
        in_specs=[SMEM] + [VMEM] * (count + 4),
        out_specs=VMEM,
        scratch_shapes=[pltpu.VMEM((NCOLOR * sites // GROUPS, 128), f32)],
        compiler_params=pltpu.CompilerParams(vmem_limit_bytes=24 * 1024 * 1024),
        name="project",
    )(index, *received, high, low, jnp.transpose(sink_noise.reshape(NEIG, NSPIN)), eig_block.reshape(1, NEIG))
    parts = lax.all_to_all(parts.reshape(times * count, 8, 128), ("tm", "slab"), split_axis=0, concat_axis=0, tiled=True)
    factor = 1.0 / math.sqrt(times * NEIG * NSPIN / NBLOCK)
    own_rows, line = pl.pallas_call(
        functools.partial(finish_kernel, count, factor),
        out_shape=(jax.ShapeDtypeStruct((COLS, per), f32), jax.ShapeDtypeStruct((2, NSPIN, NBLOCK), f32)),
        in_specs=[SMEM, VMEM],
        out_specs=(VMEM, VMEM),
        compiler_params=pltpu.CompilerParams(vmem_limit_bytes=8 * 1024 * 1024),
        name="finish",
    )(time, parts.reshape(times, count, 8, 128))
    projected = jnp.transpose(own_rows).reshape(per, 1, 2, PAIRS)
    return projected, jnp.transpose(line, (0, 2, 1))


def solution(mesh):
    in_specs = (P("tm", None, "slab"), P("tm", None, None, None, "slab"), P(None, "tm", None), P())
    out_specs = (P("slab", "tm", None, None), P())
    return jax.shard_map(body, mesh=mesh, in_specs=in_specs, out_specs=out_specs, check_vma=False)
```

```python
import functools
import math

import jax
import jax.numpy as jnp
from jax import lax
from jax.experimental import pallas as pl
from jax.experimental.pallas import tpu as pltpu
from jax.sharding import PartitionSpec as P

NSPIN = 4
NCOLOR = 3
NEIG = 192
NBLOCK = 8
PAIRS = NSPIN * NSPIN
COLS = 2 * PAIRS
GROUPS = 128 // COLS
CORES = 2
LINE_LANE = 96

ORDER = (4, 6, 5, 7, 1, 3, 2)

VMEM = pl.BlockSpec(memory_space=pltpu.VMEM)
SMEM = pl.BlockSpec(memory_space=pltpu.SMEM)


def split(value):
    high = value.astype(jnp.bfloat16)
    low = (value - high.astype(jnp.float32)).astype(jnp.bfloat16)
    return high, low


def pack_kernel(partners, index_ref, time_ref, sol_ref, *refs):
    out_refs, (tiles, turned) = refs[: len(partners)], refs[len(partners) :]
    count = len(partners)
    width = sol_ref.shape[1] // GROUPS
    rows = width // count
    per_group = width // 128
    for i in range(tiles.shape[0]):
        tiles[i] = sol_ref[:, pl.ds(128 * i, 128)]
    for color in range(NCOLOR):
        for i in range(per_group):
            stacked = jnp.concatenate(
                [tiles[g * per_group + i, pl.ds(color, COLS, stride=NCOLOR), :] for g in range(GROUPS)], axis=0
            )
            turned[pl.ds(128 * i, 128), :] = stacked.T
        for partner, out_ref in zip(partners, out_refs):
            r = jnp.bitwise_xor(index_ref[0], partner)
            out_ref[pl.ds(color * rows, rows), :] = turned[pl.ds(r, rows, stride=count), :]


def split_kernel(vec_ref, high_ref, low_ref, landed, arrived):
    width = vec_ref.shape[3] // GROUPS
    steps = [(part, color) for color in range(NCOLOR) for part in range(2)]
    copies = [
        pltpu.make_async_copy(vec_ref.at[part, color], landed.at[part, color], arrived.at[i])
        for i, (part, color) in enumerate(steps)
    ]
    for copy in copies:
        copy.start()
    for copy, (part, color) in zip(copies, steps):
        copy.wait()
        for g in range(GROUPS):
            rows = pl.ds((g * 2 + part) * NEIG, NEIG)
            lanes = pl.ds(color * width, width)
            high, low = split(landed[part, color, :, pl.ds(g * width, width)])
            high_ref[rows, lanes] = high
            low_ref[rows, lanes] = low


def project_kernel(partners, index_ref, *refs):
    count = len(partners)
    field_refs = refs[:count]
    high_ref, low_ref, noise_ref, block_ref, out_ref, line_ref, weights = refs[count:]
    width = high_ref.shape[1] // NCOLOR
    rows = width // count
    per = NEIG // count
    for partner, field_ref in zip(partners, field_refs):
        s = jnp.bitwise_xor(index_ref[0], partner)
        for color in range(NCOLOR):
            weights[pl.ds(color * width + s, rows, stride=count), :] = field_ref[pl.ds(color * rows, rows), :]
    high, low = split(weights[...].T)
    dims = (((1,), (1,)), ((), ()))
    total = jnp.zeros((COLS, 2 * NEIG), jnp.float32)
    for g in range(GROUPS):
        vecs, columns = pl.ds(g * 2 * NEIG, 2 * NEIG), slice(g * COLS, (g + 1) * COLS)
        both = jnp.concatenate([high[columns], low[columns]], axis=0)
        first = lax.dot_general(both, high_ref[vecs, :], dims, preferred_element_type=jnp.float32)
        second = lax.dot_general(high[columns], low_ref[vecs, :], dims, preferred_element_type=jnp.float32)
        total += first[:COLS] + (first[COLS:] + second)
    with_real, with_imag = total[:, :NEIG], total[:, NEIG:]
    real = with_real[:PAIRS] + with_imag[PAIRS:]
    imag = with_real[PAIRS:] - with_imag[:PAIRS]
    noise = jnp.concatenate(
        [jnp.broadcast_to(noise_ref[pl.ds(spin, 1), :], (NSPIN, NEIG)) for spin in range(NSPIN)], axis=0
    )
    zreal = (noise == 0).astype(jnp.float32) - (noise == 2).astype(jnp.float32)
    zimag = (noise == 1).astype(jnp.float32) - (noise == 3).astype(jnp.float32)
    line = jnp.concatenate([zreal * real + zimag * imag, zreal * imag - zimag * real], axis=0)
    blocks = lax.broadcasted_iota(jnp.int32, (NBLOCK, NEIG), 0)
    onehot = (blocks == block_ref[...]).astype(jnp.bfloat16)
    line_high, line_low = split(line)
    line_sum = lax.dot_general(onehot, line_high, dims, preferred_element_type=jnp.float32)
    line_sum += lax.dot_general(onehot, line_low, dims, preferred_element_type=jnp.float32)
    sums = jnp.concatenate([real, imag], axis=0)
    lines = jnp.concatenate([jnp.zeros((8, LINE_LANE), jnp.float32), line_sum], axis=1)
    line_ref[...] = lines
    for j in range(count):
        pieces = [sums[8 * i : 8 * i + 8, per * j : per * (j + 1)] for i in range(COLS // 8)]
        pieces.append(jnp.zeros((8, 128 - per * len(pieces)), jnp.float32))
        out_ref[j] = jnp.concatenate(pieces, axis=1) + lines


def join_kernel(part_ref, line_ref, out_ref):
    count = part_ref.shape[0]
    for j in range(count):
        part = part_ref[j] + line_ref[...]
        for i in range(out_ref.shape[0]):
            out_ref[i, count - 1 - j] = part


def finish_kernel(count, factor, index_ref, parts_ref, rows_ref, line_ref):
    per = NEIG // count
    own = jnp.sum(parts_ref[parts_ref.shape[0] - 1 - index_ref[0] // CORES], axis=0)
    for i in range(COLS // 8):
        rows_ref[pl.ds(8 * i, 8), :] = own[:, per * i : per * (i + 1)]
    whole = jnp.sum(jnp.sum(parts_ref[...], axis=1), axis=0)
    turned = whole.T[LINE_LANE:]
    for part in range(2):
        first = PAIRS * part
        line_ref[part] = factor * sum(turned[first + NSPIN * s : first + NSPIN * (s + 1)] for s in range(NSPIN))


def body(solutions, eigvecs, sink_noise, eig_block):
    count = lax.axis_size("slab")
    times = lax.axis_size("tm")
    sites = solutions.shape[-1]
    rows = NCOLOR * sites // GROUPS // count
    per = NEIG // count
    f32 = jnp.float32
    index = lax.axis_index("slab").reshape(1)
    time = lax.axis_index("tm").reshape(1)
    far = [p for p in ORDER if p < count]
    partners = [0] + far + [p for p in range(1, count) if p not in far]
    chunks = pl.pallas_call(
        functools.partial(pack_kernel, partners),
        out_shape=[jax.ShapeDtypeStruct((rows, 128), f32)] * count,
        in_specs=[SMEM, SMEM, VMEM],
        out_specs=[VMEM] * count,
        scratch_shapes=[pltpu.VMEM((sites // 128, NCOLOR * COLS, 128), f32), pltpu.VMEM((sites // GROUPS, 128), f32)],
        compiler_params=pltpu.CompilerParams(vmem_limit_bytes=8 * 1024 * 1024),
        name="pack",
    )(index, time, solutions.reshape(solutions.shape[1:]))
    received = [
        lax.ppermute(chunk, "slab", [(i, i ^ partner) for i in range(count)]) if partner else chunk
        for partner, chunk in zip(partners, chunks)
    ]
    vectors = jnp.transpose(eigvecs.reshape(eigvecs.shape[1:]), (0, 2, 1, 3))
    shape = jax.ShapeDtypeStruct((2 * GROUPS * NEIG, NCOLOR * sites // GROUPS), jnp.bfloat16)
    high, low = pl.pallas_call(
        split_kernel,
        out_shape=(shape, shape),
        in_specs=[pl.BlockSpec(memory_space=pltpu.HBM)],
        out_specs=(VMEM, VMEM),
        scratch_shapes=[pltpu.VMEM(vectors.shape, f32), pltpu.SemaphoreType.DMA((2 * NCOLOR,))],
        compiler_params=pltpu.CompilerParams(vmem_limit_bytes=24 * 1024 * 1024),
        cost_estimate=pl.CostEstimate(flops=6 * eigvecs.size, bytes_accessed=8 * eigvecs.size, transcendentals=0),
        name="split",
    )(pltpu.with_memory_space_constraint(vectors, pltpu.HBM))
    part, line = pl.pallas_call(
        functools.partial(project_kernel, partners),
        out_shape=(pltpu.VMEM((count, 8, 128), f32), pltpu.VMEM((8, 128), f32)),
        in_specs=[SMEM] + [VMEM] * (count + 4),
        out_specs=(VMEM, VMEM),
        scratch_shapes=[pltpu.VMEM((NCOLOR * sites // GROUPS, 128), f32)],
        compiler_params=pltpu.CompilerParams(vmem_limit_bytes=24 * 1024 * 1024),
        name="project",
    )(index, *received, high, low, jnp.transpose(sink_noise.reshape(NEIG, NSPIN)), eig_block.reshape(1, NEIG))
    line = lax.ppermute(line, "tm", [(i, i ^ 1) for i in range(times)])
    chips = times // CORES
    parts = pl.pallas_call(
        join_kernel,
        out_shape=pltpu.VMEM((chips, count, 8, 128), f32),
        in_specs=[VMEM, VMEM],
        out_specs=VMEM,
        compiler_params=pltpu.CompilerParams(vmem_limit_bytes=8 * 1024 * 1024),
        name="join",
    )(part, line)
    groups = [
        [(chip * CORES + core) * count + s for chip in reversed(range(chips)) for s in reversed(range(count))]
        for core in range(CORES)
    ]
    parts = lax.all_to_all(
        parts.reshape(chips * count, 8, 128), ("tm", "slab"), 0, 0, axis_index_groups=groups, tiled=True
    )
    factor = 1.0 / math.sqrt(times * NEIG * NSPIN / NBLOCK)
    own_rows, line = pl.pallas_call(
        functools.partial(finish_kernel, count, factor),
        out_shape=(jax.ShapeDtypeStruct((COLS, per), f32), jax.ShapeDtypeStruct((2, NSPIN, NBLOCK), f32)),
        in_specs=[SMEM, VMEM],
        out_specs=(VMEM, VMEM),
        compiler_params=pltpu.CompilerParams(vmem_limit_bytes=8 * 1024 * 1024),
        name="finish",
    )(time, parts.reshape(chips, count, 8, 128))
    projected = jnp.transpose(own_rows).reshape(per, 1, 2, PAIRS)
    return projected, jnp.transpose(line, (0, 2, 1))


def solution(mesh):
    in_specs = (P("tm", None, "slab"), P("tm", None, None, None, "slab"), P(None, "tm", None), P())
    out_specs = (P("slab", "tm", None, None), P())
    return jax.shard_map(body, mesh=mesh, in_specs=in_specs, out_specs=out_specs, check_vma=False)
```

```python
import functools
import math

import jax
import jax.numpy as jnp
from jax import lax
from jax.experimental import pallas as pl
from jax.experimental.pallas import tpu as pltpu
from jax.sharding import PartitionSpec as P

NSPIN = 4
NCOLOR = 3
NEIG = 192
NBLOCK = 8
PAIRS = NSPIN * NSPIN
COLS = 2 * PAIRS
GROUPS = 128 // COLS
CORES = 2
LINE_LANE = 96

ORDER = (4, 1, 6, 5, 7, 3, 2)

VMEM = pl.BlockSpec(memory_space=pltpu.VMEM)
SMEM = pl.BlockSpec(memory_space=pltpu.SMEM)


def split(value):
    high = value.astype(jnp.bfloat16)
    low = (value - high.astype(jnp.float32)).astype(jnp.bfloat16)
    return high, low


def pack_kernel(partners, index_ref, time_ref, sol_ref, *refs):
    out_refs, (tiles, turned) = refs[: len(partners)], refs[len(partners) :]
    count = len(partners)
    width = sol_ref.shape[1] // GROUPS
    rows = width // count
    per_group = width // 128
    for i in range(tiles.shape[0]):
        tiles[i] = sol_ref[:, pl.ds(128 * i, 128)]
    for color in range(NCOLOR):
        for i in range(per_group):
            stacked = jnp.concatenate(
                [tiles[g * per_group + i, pl.ds(color, COLS, stride=NCOLOR), :] for g in range(GROUPS)], axis=0
            )
            turned[pl.ds(128 * i, 128), :] = stacked.T
        for partner, out_ref in zip(partners, out_refs):
            r = jnp.bitwise_xor(index_ref[0], partner)
            out_ref[pl.ds(color * rows, rows), :] = turned[pl.ds(r, rows, stride=count), :]


def split_kernel(vec_ref, high_ref, low_ref, landed, arrived):
    width = vec_ref.shape[3] // GROUPS
    steps = [(part, color) for color in range(NCOLOR) for part in range(2)]
    copies = [
        pltpu.make_async_copy(vec_ref.at[part, color], landed.at[part, color], arrived.at[i])
        for i, (part, color) in enumerate(steps)
    ]
    for copy in copies:
        copy.start()
    for copy, (part, color) in zip(copies, steps):
        copy.wait()
        for g in range(GROUPS):
            rows = pl.ds((g * 2 + part) * NEIG, NEIG)
            lanes = pl.ds(color * width, width)
            high, low = split(landed[part, color, :, pl.ds(g * width, width)])
            high_ref[rows, lanes] = high
            low_ref[rows, lanes] = low


def project_kernel(partners, index_ref, *refs):
    count = len(partners)
    field_refs = refs[:count]
    high_ref, low_ref, noise_ref, block_ref, out_ref, line_ref, weights = refs[count:]
    width = high_ref.shape[1] // NCOLOR
    rows = width // count
    per = NEIG // count
    for partner, field_ref in zip(partners, field_refs):
        s = jnp.bitwise_xor(index_ref[0], partner)
        for color in range(NCOLOR):
            weights[pl.ds(color * width + s, rows, stride=count), :] = field_ref[pl.ds(color * rows, rows), :]
    high, low = split(weights[...].T)
    dims = (((1,), (1,)), ((), ()))
    total = jnp.zeros((COLS, 2 * NEIG), jnp.float32)
    for g in range(GROUPS):
        vecs, columns = pl.ds(g * 2 * NEIG, 2 * NEIG), slice(g * COLS, (g + 1) * COLS)
        both = jnp.concatenate([high[columns], low[columns]], axis=0)
        first = lax.dot_general(both, high_ref[vecs, :], dims, preferred_element_type=jnp.float32)
        second = lax.dot_general(high[columns], low_ref[vecs, :], dims, preferred_element_type=jnp.float32)
        total += first[:COLS] + (first[COLS:] + second)
    with_real, with_imag = total[:, :NEIG], total[:, NEIG:]
    real = with_real[:PAIRS] + with_imag[PAIRS:]
    imag = with_real[PAIRS:] - with_imag[:PAIRS]
    noise = jnp.concatenate(
        [jnp.broadcast_to(noise_ref[pl.ds(spin, 1), :], (NSPIN, NEIG)) for spin in range(NSPIN)], axis=0
    )
    zreal = (noise == 0).astype(jnp.float32) - (noise == 2).astype(jnp.float32)
    zimag = (noise == 1).astype(jnp.float32) - (noise == 3).astype(jnp.float32)
    line = jnp.concatenate([zreal * real + zimag * imag, zreal * imag - zimag * real], axis=0)
    blocks = lax.broadcasted_iota(jnp.int32, (NBLOCK, NEIG), 0)
    onehot = (blocks == block_ref[...]).astype(jnp.bfloat16)
    line_high, line_low = split(line)
    line_sum = lax.dot_general(onehot, line_high, dims, preferred_element_type=jnp.float32)
    line_sum += lax.dot_general(onehot, line_low, dims, preferred_element_type=jnp.float32)
    sums = jnp.concatenate([real, imag], axis=0)
    lines = jnp.concatenate([jnp.zeros((8, LINE_LANE), jnp.float32), line_sum], axis=1)
    line_ref[...] = lines
    for j in range(count):
        pieces = [sums[8 * i : 8 * i + 8, per * j : per * (j + 1)] for i in range(COLS // 8)]
        pieces.append(jnp.zeros((8, 128 - per * len(pieces)), jnp.float32))
        out_ref[j] = jnp.concatenate(pieces, axis=1) + lines


def join_kernel(part_ref, line_ref, out_ref):
    count = part_ref.shape[0]
    for j in range(count):
        part = part_ref[j] + line_ref[...]
        for i in range(out_ref.shape[0]):
            out_ref[i, count - 1 - j] = part


def finish_kernel(count, factor, index_ref, parts_ref, rows_ref, line_ref):
    per = NEIG // count
    own = jnp.sum(parts_ref[parts_ref.shape[0] - 1 - index_ref[0] // CORES], axis=0)
    for i in range(COLS // 8):
        rows_ref[pl.ds(8 * i, 8), :] = own[:, per * i : per * (i + 1)]
    whole = jnp.sum(jnp.sum(parts_ref[...], axis=1), axis=0)
    turned = whole.T[LINE_LANE:]
    for part in range(2):
        first = PAIRS * part
        line_ref[part] = factor * sum(turned[first + NSPIN * s : first + NSPIN * (s + 1)] for s in range(NSPIN))


def body(solutions, eigvecs, sink_noise, eig_block):
    count = lax.axis_size("slab")
    times = lax.axis_size("tm")
    sites = solutions.shape[-1]
    rows = NCOLOR * sites // GROUPS // count
    per = NEIG // count
    f32 = jnp.float32
    index = lax.axis_index("slab").reshape(1)
    time = lax.axis_index("tm").reshape(1)
    far = [p for p in ORDER if p < count]
    partners = [0] + far + [p for p in range(1, count) if p not in far]
    chunks = pl.pallas_call(
        functools.partial(pack_kernel, partners),
        out_shape=[jax.ShapeDtypeStruct((rows, 128), f32)] * count,
        in_specs=[SMEM, SMEM, VMEM],
        out_specs=[VMEM] * count,
        scratch_shapes=[pltpu.VMEM((sites // 128, NCOLOR * COLS, 128), f32), pltpu.VMEM((sites // GROUPS, 128), f32)],
        compiler_params=pltpu.CompilerParams(vmem_limit_bytes=8 * 1024 * 1024),
        name="pack",
    )(index, time, solutions.reshape(solutions.shape[1:]))
    received = [
        lax.ppermute(chunk, "slab", [(i, i ^ partner) for i in range(count)]) if partner else chunk
        for partner, chunk in zip(partners, chunks)
    ]
    vectors = jnp.transpose(eigvecs.reshape(eigvecs.shape[1:]), (0, 2, 1, 3))
    shape = jax.ShapeDtypeStruct((2 * GROUPS * NEIG, NCOLOR * sites // GROUPS), jnp.bfloat16)
    high, low = pl.pallas_call(
        split_kernel,
        out_shape=(shape, shape),
        in_specs=[pl.BlockSpec(memory_space=pltpu.HBM)],
        out_specs=(VMEM, VMEM),
        scratch_shapes=[pltpu.VMEM(vectors.shape, f32), pltpu.SemaphoreType.DMA((2 * NCOLOR,))],
        compiler_params=pltpu.CompilerParams(vmem_limit_bytes=24 * 1024 * 1024),
        cost_estimate=pl.CostEstimate(flops=6 * eigvecs.size, bytes_accessed=8 * eigvecs.size, transcendentals=0),
        name="split",
    )(pltpu.with_memory_space_constraint(vectors, pltpu.HBM))
    part, line = pl.pallas_call(
        functools.partial(project_kernel, partners),
        out_shape=(pltpu.VMEM((count, 8, 128), f32), pltpu.VMEM((8, 128), f32)),
        in_specs=[SMEM] + [VMEM] * (count + 4),
        out_specs=(VMEM, VMEM),
        scratch_shapes=[pltpu.VMEM((NCOLOR * sites // GROUPS, 128), f32)],
        compiler_params=pltpu.CompilerParams(vmem_limit_bytes=24 * 1024 * 1024),
        name="project",
    )(index, *received, high, low, jnp.transpose(sink_noise.reshape(NEIG, NSPIN)), eig_block.reshape(1, NEIG))
    line = lax.ppermute(line, "tm", [(i, i ^ 1) for i in range(times)])
    chips = times // CORES
    parts = pl.pallas_call(
        join_kernel,
        out_shape=pltpu.VMEM((chips, count, 8, 128), f32),
        in_specs=[VMEM, VMEM],
        out_specs=VMEM,
        compiler_params=pltpu.CompilerParams(vmem_limit_bytes=8 * 1024 * 1024),
        name="join",
    )(part, line)
    groups = [
        [(chip * CORES + core) * count + s for chip in reversed(range(chips)) for s in reversed(range(count))]
        for core in range(CORES)
    ]
    parts = lax.all_to_all(
        parts.reshape(chips * count, 8, 128), ("tm", "slab"), 0, 0, axis_index_groups=groups, tiled=True
    )
    factor = 1.0 / math.sqrt(times * NEIG * NSPIN / NBLOCK)
    own_rows, line = pl.pallas_call(
        functools.partial(finish_kernel, count, factor),
        out_shape=(jax.ShapeDtypeStruct((COLS, per), f32), jax.ShapeDtypeStruct((2, NSPIN, NBLOCK), f32)),
        in_specs=[SMEM, VMEM],
        out_specs=(VMEM, VMEM),
        compiler_params=pltpu.CompilerParams(vmem_limit_bytes=8 * 1024 * 1024),
        name="finish",
    )(time, parts.reshape(chips, count, 8, 128))
    projected = jnp.transpose(own_rows).reshape(per, 1, 2, PAIRS)
    return projected, jnp.transpose(line, (0, 2, 1))


def solution(mesh):
    in_specs = (P("tm", None, "slab"), P("tm", None, None, None, "slab"), P(None, "tm", None), P())
    out_specs = (P("slab", "tm", None, None), P())
    return jax.shard_map(body, mesh=mesh, in_specs=in_specs, out_specs=out_specs, check_vma=False)
```

```python
import functools
import math

import jax
import jax.numpy as jnp
from jax import lax
from jax.experimental import pallas as pl
from jax.experimental.pallas import tpu as pltpu
from jax.sharding import PartitionSpec as P

NSPIN = 4
NCOLOR = 3
NEIG = 192
NBLOCK = 8
PAIRS = NSPIN * NSPIN
COLS = 2 * PAIRS
GROUPS = 128 // COLS
CORES = 2
LINE_LANE = 96

ORDER = (4, 3, 6, 5, 7, 2, 1)

VMEM = pl.BlockSpec(memory_space=pltpu.VMEM)
SMEM = pl.BlockSpec(memory_space=pltpu.SMEM)


def split(value):
    high = value.astype(jnp.bfloat16)
    low = (value - high.astype(jnp.float32)).astype(jnp.bfloat16)
    return high, low


def pack_kernel(partners, index_ref, time_ref, sol_ref, *refs):
    out_refs, (tiles, turned) = refs[: len(partners)], refs[len(partners) :]
    count = len(partners)
    width = sol_ref.shape[1] // GROUPS
    rows = width // count
    per_group = width // 128
    for i in range(tiles.shape[0]):
        tiles[i] = sol_ref[:, pl.ds(128 * i, 128)]
    for color in range(NCOLOR):
        for i in range(per_group):
            stacked = jnp.concatenate(
                [tiles[g * per_group + i, pl.ds(color, COLS, stride=NCOLOR), :] for g in range(GROUPS)], axis=0
            )
            turned[pl.ds(128 * i, 128), :] = stacked.T
        for partner, out_ref in zip(partners, out_refs):
            r = jnp.bitwise_xor(index_ref[0], partner)
            out_ref[pl.ds(color * rows, rows), :] = turned[pl.ds(r, rows, stride=count), :]


def split_kernel(vec_ref, high_ref, low_ref, landed, arrived):
    width = vec_ref.shape[3] // GROUPS
    steps = [(part, color) for color in range(NCOLOR) for part in range(2)]
    copies = [
        pltpu.make_async_copy(vec_ref.at[part, color], landed.at[part, color], arrived.at[i])
        for i, (part, color) in enumerate(steps)
    ]
    for copy in copies:
        copy.start()
    for copy, (part, color) in zip(copies, steps):
        copy.wait()
        for g in range(GROUPS):
            rows = pl.ds((g * 2 + part) * NEIG, NEIG)
            lanes = pl.ds(color * width, width)
            high, low = split(landed[part, color, :, pl.ds(g * width, width)])
            high_ref[rows, lanes] = high
            low_ref[rows, lanes] = low


def project_kernel(partners, index_ref, *refs):
    count = len(partners)
    field_refs = refs[:count]
    high_ref, low_ref, noise_ref, block_ref, out_ref, line_ref, weights = refs[count:]
    width = high_ref.shape[1] // NCOLOR
    rows = width // count
    per = NEIG // count
    for partner, field_ref in zip(partners, field_refs):
        s = jnp.bitwise_xor(index_ref[0], partner)
        for color in range(NCOLOR):
            weights[pl.ds(color * width + s, rows, stride=count), :] = field_ref[pl.ds(color * rows, rows), :]
    high, low = split(weights[...].T)
    dims = (((1,), (1,)), ((), ()))
    total = jnp.zeros((COLS, 2 * NEIG), jnp.float32)
    for g in range(GROUPS):
        vecs, columns = pl.ds(g * 2 * NEIG, 2 * NEIG), slice(g * COLS, (g + 1) * COLS)
        both = jnp.concatenate([high[columns], low[columns]], axis=0)
        first = lax.dot_general(both, high_ref[vecs, :], dims, preferred_element_type=jnp.float32)
        second = lax.dot_general(high[columns], low_ref[vecs, :], dims, preferred_element_type=jnp.float32)
        total += first[:COLS] + (first[COLS:] + second)
    with_real, with_imag = total[:, :NEIG], total[:, NEIG:]
    real = with_real[:PAIRS] + with_imag[PAIRS:]
    imag = with_real[PAIRS:] - with_imag[:PAIRS]
    noise = jnp.concatenate(
        [jnp.broadcast_to(noise_ref[pl.ds(spin, 1), :], (NSPIN, NEIG)) for spin in range(NSPIN)], axis=0
    )
    zreal = (noise == 0).astype(jnp.float32) - (noise == 2).astype(jnp.float32)
    zimag = (noise == 1).astype(jnp.float32) - (noise == 3).astype(jnp.float32)
    line = jnp.concatenate([zreal * real + zimag * imag, zreal * imag - zimag * real], axis=0)
    blocks = lax.broadcasted_iota(jnp.int32, (NBLOCK, NEIG), 0)
    onehot = (blocks == block_ref[...]).astype(jnp.bfloat16)
    line_high, line_low = split(line)
    line_sum = lax.dot_general(onehot, line_high, dims, preferred_element_type=jnp.float32)
    line_sum += lax.dot_general(onehot, line_low, dims, preferred_element_type=jnp.float32)
    sums = jnp.concatenate([real, imag], axis=0)
    lines = jnp.concatenate([jnp.zeros((8, LINE_LANE), jnp.float32), line_sum], axis=1)
    line_ref[...] = lines
    for j in range(count):
        pieces = [sums[8 * i : 8 * i + 8, per * j : per * (j + 1)] for i in range(COLS // 8)]
        pieces.append(jnp.zeros((8, 128 - per * len(pieces)), jnp.float32))
        out_ref[j] = jnp.concatenate(pieces, axis=1) + lines


def join_kernel(part_ref, line_ref, out_ref):
    count = part_ref.shape[0]
    for j in range(count):
        part = part_ref[j] + line_ref[...]
        for i in range(out_ref.shape[0]):
            out_ref[i, count - 1 - j] = part


def finish_kernel(count, factor, index_ref, parts_ref, rows_ref, line_ref):
    per = NEIG // count
    own = jnp.sum(parts_ref[parts_ref.shape[0] - 1 - index_ref[0] // CORES], axis=0)
    for i in range(COLS // 8):
        rows_ref[pl.ds(8 * i, 8), :] = own[:, per * i : per * (i + 1)]
    whole = jnp.sum(jnp.sum(parts_ref[...], axis=1), axis=0)
    turned = whole.T[LINE_LANE:]
    for part in range(2):
        first = PAIRS * part
        line_ref[part] = factor * sum(turned[first + NSPIN * s : first + NSPIN * (s + 1)] for s in range(NSPIN))


def body(solutions, eigvecs, sink_noise, eig_block):
    count = lax.axis_size("slab")
    times = lax.axis_size("tm")
    sites = solutions.shape[-1]
    rows = NCOLOR * sites // GROUPS // count
    per = NEIG // count
    f32 = jnp.float32
    index = lax.axis_index("slab").reshape(1)
    time = lax.axis_index("tm").reshape(1)
    far = [p for p in ORDER if p < count]
    partners = [0] + far + [p for p in range(1, count) if p not in far]
    chunks = pl.pallas_call(
        functools.partial(pack_kernel, partners),
        out_shape=[jax.ShapeDtypeStruct((rows, 128), f32)] * count,
        in_specs=[SMEM, SMEM, VMEM],
        out_specs=[VMEM] * count,
        scratch_shapes=[pltpu.VMEM((sites // 128, NCOLOR * COLS, 128), f32), pltpu.VMEM((sites // GROUPS, 128), f32)],
        compiler_params=pltpu.CompilerParams(vmem_limit_bytes=8 * 1024 * 1024),
        name="pack",
    )(index, time, solutions.reshape(solutions.shape[1:]))
    received = [
        lax.ppermute(chunk, "slab", [(i, i ^ partner) for i in range(count)]) if partner else chunk
        for partner, chunk in zip(partners, chunks)
    ]
    vectors = jnp.transpose(eigvecs.reshape(eigvecs.shape[1:]), (0, 2, 1, 3))
    shape = jax.ShapeDtypeStruct((2 * GROUPS * NEIG, NCOLOR * sites // GROUPS), jnp.bfloat16)
    high, low = pl.pallas_call(
        split_kernel,
        out_shape=(shape, shape),
        in_specs=[pl.BlockSpec(memory_space=pltpu.HBM)],
        out_specs=(VMEM, VMEM),
        scratch_shapes=[pltpu.VMEM(vectors.shape, f32), pltpu.SemaphoreType.DMA((2 * NCOLOR,))],
        compiler_params=pltpu.CompilerParams(vmem_limit_bytes=24 * 1024 * 1024),
        cost_estimate=pl.CostEstimate(flops=6 * eigvecs.size, bytes_accessed=8 * eigvecs.size, transcendentals=0),
        name="split",
    )(pltpu.with_memory_space_constraint(vectors, pltpu.HBM))
    part, line = pl.pallas_call(
        functools.partial(project_kernel, partners),
        out_shape=(pltpu.VMEM((count, 8, 128), f32), pltpu.VMEM((8, 128), f32)),
        in_specs=[SMEM] + [VMEM] * (count + 4),
        out_specs=(VMEM, VMEM),
        scratch_shapes=[pltpu.VMEM((NCOLOR * sites // GROUPS, 128), f32)],
        compiler_params=pltpu.CompilerParams(vmem_limit_bytes=24 * 1024 * 1024),
        name="project",
    )(index, *received, high, low, jnp.transpose(sink_noise.reshape(NEIG, NSPIN)), eig_block.reshape(1, NEIG))
    line = lax.ppermute(line, "tm", [(i, i ^ 1) for i in range(times)])
    chips = times // CORES
    parts = pl.pallas_call(
        join_kernel,
        out_shape=pltpu.VMEM((chips, count, 8, 128), f32),
        in_specs=[VMEM, VMEM],
        out_specs=VMEM,
        compiler_params=pltpu.CompilerParams(vmem_limit_bytes=8 * 1024 * 1024),
        name="join",
    )(part, line)
    groups = [
        [(chip * CORES + core) * count + s for chip in reversed(range(chips)) for s in reversed(range(count))]
        for core in range(CORES)
    ]
    parts = lax.all_to_all(
        parts.reshape(chips * count, 8, 128), ("tm", "slab"), 0, 0, axis_index_groups=groups, tiled=True
    )
    factor = 1.0 / math.sqrt(times * NEIG * NSPIN / NBLOCK)
    own_rows, line = pl.pallas_call(
        functools.partial(finish_kernel, count, factor),
        out_shape=(jax.ShapeDtypeStruct((COLS, per), f32), jax.ShapeDtypeStruct((2, NSPIN, NBLOCK), f32)),
        in_specs=[SMEM, VMEM],
        out_specs=(VMEM, VMEM),
        compiler_params=pltpu.CompilerParams(vmem_limit_bytes=8 * 1024 * 1024),
        name="finish",
    )(time, parts.reshape(chips, count, 8, 128))
    projected = jnp.transpose(own_rows).reshape(per, 1, 2, PAIRS)
    return projected, jnp.transpose(line, (0, 2, 1))


def solution(mesh):
    in_specs = (P("tm", None, "slab"), P("tm", None, None, None, "slab"), P(None, "tm", None), P())
    out_specs = (P("slab", "tm", None, None), P())
    return jax.shard_map(body, mesh=mesh, in_specs=in_specs, out_specs=out_specs, check_vma=False)
```

```python
import functools
import math

import jax
import jax.numpy as jnp
from jax import lax
from jax.experimental import pallas as pl
from jax.experimental.pallas import tpu as pltpu
from jax.sharding import PartitionSpec as P

NSPIN = 4
NCOLOR = 3
NEIG = 192
NBLOCK = 8
PAIRS = NSPIN * NSPIN
COLS = 2 * PAIRS
GROUPS = 128 // COLS
CORES = 2
LINE_LANE = 96

ORDER = (4, 3, 6, 5, 7, 2, 1)

VMEM = pl.BlockSpec(memory_space=pltpu.VMEM)
SMEM = pl.BlockSpec(memory_space=pltpu.SMEM)


def split(value):
    high = value.astype(jnp.bfloat16)
    low = (value - high.astype(jnp.float32)).astype(jnp.bfloat16)
    return high, low


def pack_kernel(partners, index_ref, time_ref, sol_ref, *refs):
    out_refs, (tiles, turned) = refs[: len(partners)], refs[len(partners) :]
    count = len(partners)
    width = sol_ref.shape[1] // GROUPS
    rows = width // count
    per_group = width // 128
    for i in range(tiles.shape[0]):
        tiles[i] = sol_ref[:, pl.ds(128 * i, 128)]
    for color in range(NCOLOR):
        for i in range(per_group):
            stacked = jnp.concatenate(
                [tiles[g * per_group + i, pl.ds(color, COLS, stride=NCOLOR), :] for g in range(GROUPS)], axis=0
            )
            turned[pl.ds(128 * i, 128), :] = stacked.T
        for partner, out_ref in zip(partners, out_refs):
            r = jnp.bitwise_xor(index_ref[0], partner)
            out_ref[pl.ds(color * rows, rows), :] = turned[pl.ds(r, rows, stride=count), :]


def split_kernel(vec_ref, high_ref, low_ref, landed, arrived):
    width = vec_ref.shape[3] // GROUPS
    steps = [(part, color) for color in range(NCOLOR) for part in range(2)]
    copies = [
        pltpu.make_async_copy(vec_ref.at[part, color], landed.at[part, color], arrived.at[i])
        for i, (part, color) in enumerate(steps)
    ]
    for copy in copies:
        copy.start()
    for color in range(NCOLOR):
        for copy in copies[2 * color : 2 * color + 2]:
            copy.wait()
        for g in range(GROUPS):
            rows = pl.ds((g * NCOLOR + color) * width, width)
            both = jnp.concatenate([landed[part, color, :, pl.ds(g * width, width)] for part in range(2)], axis=0)
            high, low = split(both.T)
            high_ref[rows, :] = high
            low_ref[rows, :] = low


def project_kernel(partners, index_ref, *refs):
    count = len(partners)
    field_refs = refs[:count]
    high_ref, low_ref, noise_ref, block_ref, out_ref, line_ref, weights = refs[count:]
    width = high_ref.shape[0] // (GROUPS * NCOLOR)
    rows = width // count
    per = NEIG // count
    for partner, field_ref in zip(partners, field_refs):
        s = jnp.bitwise_xor(index_ref[0], partner)
        for color in range(NCOLOR):
            weights[pl.ds(color * width + s, rows, stride=count), :] = field_ref[pl.ds(color * rows, rows), :]
    high, low = split(weights[...].T)
    dims = (((1,), (1,)), ((), ()))
    total = jnp.zeros((COLS, 2 * NEIG), jnp.float32)
    for g in range(GROUPS):
        vecs, columns = pl.ds(g * NCOLOR * width, NCOLOR * width), slice(g * COLS, (g + 1) * COLS)
        both = jnp.concatenate([high[columns], low[columns]], axis=0)
        first = jnp.dot(both, high_ref[vecs, :], preferred_element_type=jnp.float32)
        second = jnp.dot(high[columns], low_ref[vecs, :], preferred_element_type=jnp.float32)
        total += first[:COLS] + (first[COLS:] + second)
    with_real, with_imag = total[:, :NEIG], total[:, NEIG:]
    real = with_real[:PAIRS] + with_imag[PAIRS:]
    imag = with_real[PAIRS:] - with_imag[:PAIRS]
    noise = jnp.concatenate(
        [jnp.broadcast_to(noise_ref[pl.ds(spin, 1), :], (NSPIN, NEIG)) for spin in range(NSPIN)], axis=0
    )
    zreal = (noise == 0).astype(jnp.float32) - (noise == 2).astype(jnp.float32)
    zimag = (noise == 1).astype(jnp.float32) - (noise == 3).astype(jnp.float32)
    line = jnp.concatenate([zreal * real + zimag * imag, zreal * imag - zimag * real], axis=0)
    blocks = lax.broadcasted_iota(jnp.int32, (NBLOCK, NEIG), 0)
    onehot = (blocks == block_ref[...]).astype(jnp.bfloat16)
    line_high, line_low = split(line)
    line_sum = lax.dot_general(onehot, line_high, dims, preferred_element_type=jnp.float32)
    line_sum += lax.dot_general(onehot, line_low, dims, preferred_element_type=jnp.float32)
    sums = jnp.concatenate([real, imag], axis=0)
    lines = jnp.concatenate([jnp.zeros((8, LINE_LANE), jnp.float32), line_sum], axis=1)
    line_ref[...] = lines
    for j in range(count):
        pieces = [sums[8 * i : 8 * i + 8, per * j : per * (j + 1)] for i in range(COLS // 8)]
        pieces.append(jnp.zeros((8, 128 - per * len(pieces)), jnp.float32))
        out_ref[j] = jnp.concatenate(pieces, axis=1) + lines


def join_kernel(part_ref, line_ref, out_ref):
    count = part_ref.shape[0]
    for j in range(count):
        part = part_ref[j] + line_ref[...]
        for i in range(out_ref.shape[0]):
            out_ref[i, count - 1 - j] = part


def finish_kernel(count, factor, index_ref, parts_ref, rows_ref, line_ref):
    per = NEIG // count
    own = jnp.sum(parts_ref[parts_ref.shape[0] - 1 - index_ref[0] // CORES], axis=0)
    for i in range(COLS // 8):
        rows_ref[pl.ds(8 * i, 8), :] = own[:, per * i : per * (i + 1)]
    whole = jnp.sum(jnp.sum(parts_ref[...], axis=1), axis=0)
    turned = whole.T[LINE_LANE:]
    for part in range(2):
        first = PAIRS * part
        line_ref[part] = factor * sum(turned[first + NSPIN * s : first + NSPIN * (s + 1)] for s in range(NSPIN))


def body(solutions, eigvecs, sink_noise, eig_block):
    count = lax.axis_size("slab")
    times = lax.axis_size("tm")
    sites = solutions.shape[-1]
    rows = NCOLOR * sites // GROUPS // count
    per = NEIG // count
    f32 = jnp.float32
    index = lax.axis_index("slab").reshape(1)
    time = lax.axis_index("tm").reshape(1)
    far = [p for p in ORDER if p < count]
    partners = [0] + far + [p for p in range(1, count) if p not in far]
    chunks = pl.pallas_call(
        functools.partial(pack_kernel, partners),
        out_shape=[jax.ShapeDtypeStruct((rows, 128), f32)] * count,
        in_specs=[SMEM, SMEM, VMEM],
        out_specs=[VMEM] * count,
        scratch_shapes=[pltpu.VMEM((sites // 128, NCOLOR * COLS, 128), f32), pltpu.VMEM((sites // GROUPS, 128), f32)],
        compiler_params=pltpu.CompilerParams(vmem_limit_bytes=8 * 1024 * 1024),
        name="pack",
    )(index, time, solutions.reshape(solutions.shape[1:]))
    received = [
        lax.ppermute(chunk, "slab", [(i, i ^ partner) for i in range(count)]) if partner else chunk
        for partner, chunk in zip(partners, chunks)
    ]
    vectors = jnp.transpose(eigvecs.reshape(eigvecs.shape[1:]), (0, 2, 1, 3))
    shape = jax.ShapeDtypeStruct((NCOLOR * sites, 2 * NEIG), jnp.bfloat16)
    high, low = pl.pallas_call(
        split_kernel,
        out_shape=(shape, shape),
        in_specs=[pl.BlockSpec(memory_space=pltpu.HBM)],
        out_specs=(VMEM, VMEM),
        scratch_shapes=[pltpu.VMEM(vectors.shape, f32), pltpu.SemaphoreType.DMA((2 * NCOLOR,))],
        compiler_params=pltpu.CompilerParams(vmem_limit_bytes=24 * 1024 * 1024),
        cost_estimate=pl.CostEstimate(flops=6 * eigvecs.size, bytes_accessed=8 * eigvecs.size, transcendentals=0),
        name="split",
    )(pltpu.with_memory_space_constraint(vectors, pltpu.HBM))
    part, line = pl.pallas_call(
        functools.partial(project_kernel, partners),
        out_shape=(pltpu.VMEM((count, 8, 128), f32), pltpu.VMEM((8, 128), f32)),
        in_specs=[SMEM] + [VMEM] * (count + 4),
        out_specs=(VMEM, VMEM),
        scratch_shapes=[pltpu.VMEM((NCOLOR * sites // GROUPS, 128), f32)],
        compiler_params=pltpu.CompilerParams(vmem_limit_bytes=24 * 1024 * 1024),
        name="project",
    )(index, *received, high, low, jnp.transpose(sink_noise.reshape(NEIG, NSPIN)), eig_block.reshape(1, NEIG))
    line = lax.ppermute(line, "tm", [(i, i ^ 1) for i in range(times)])
    chips = times // CORES
    parts = pl.pallas_call(
        join_kernel,
        out_shape=pltpu.VMEM((chips, count, 8, 128), f32),
        in_specs=[VMEM, VMEM],
        out_specs=VMEM,
        compiler_params=pltpu.CompilerParams(vmem_limit_bytes=8 * 1024 * 1024),
        name="join",
    )(part, line)
    groups = [
        [(chip * CORES + core) * count + s for chip in reversed(range(chips)) for s in reversed(range(count))]
        for core in range(CORES)
    ]
    parts = lax.all_to_all(
        parts.reshape(chips * count, 8, 128), ("tm", "slab"), 0, 0, axis_index_groups=groups, tiled=True
    )
    factor = 1.0 / math.sqrt(times * NEIG * NSPIN / NBLOCK)
    own_rows, line = pl.pallas_call(
        functools.partial(finish_kernel, count, factor),
        out_shape=(jax.ShapeDtypeStruct((COLS, per), f32), jax.ShapeDtypeStruct((2, NSPIN, NBLOCK), f32)),
        in_specs=[SMEM, VMEM],
        out_specs=(VMEM, VMEM),
        compiler_params=pltpu.CompilerParams(vmem_limit_bytes=8 * 1024 * 1024),
        name="finish",
    )(time, parts.reshape(chips, count, 8, 128))
    projected = jnp.transpose(own_rows).reshape(per, 1, 2, PAIRS)
    return projected, jnp.transpose(line, (0, 2, 1))


def solution(mesh):
    in_specs = (P("tm", None, "slab"), P("tm", None, None, None, "slab"), P(None, "tm", None), P())
    out_specs = (P("slab", "tm", None, None), P())
    return jax.shard_map(body, mesh=mesh, in_specs=in_specs, out_specs=out_specs, check_vma=False)
```

```python
import functools
import math

import jax
import jax.numpy as jnp
from jax import lax
from jax.experimental import pallas as pl
from jax.experimental.pallas import tpu as pltpu
from jax.sharding import PartitionSpec as P

NSPIN = 4
NCOLOR = 3
NEIG = 192
NBLOCK = 8
PAIRS = NSPIN * NSPIN
COLS = 2 * PAIRS
GROUPS = 128 // COLS
CORES = 2
LINE_LANE = 96

ORDER = (4, 3, 6, 5, 7, 2, 1)

VMEM = pl.BlockSpec(memory_space=pltpu.VMEM)
SMEM = pl.BlockSpec(memory_space=pltpu.SMEM)


def split(value):
    high = value.astype(jnp.bfloat16)
    low = (value - high.astype(jnp.float32)).astype(jnp.bfloat16)
    return high, low


def pack_kernel(partners, index_ref, time_ref, sol_ref, *refs):
    out_refs, (tiles, turned) = refs[: len(partners)], refs[len(partners) :]
    count = len(partners)
    width = sol_ref.shape[1] // GROUPS
    rows = width // count
    per_group = width // 128
    for i in range(tiles.shape[0]):
        tiles[i] = sol_ref[:, pl.ds(128 * i, 128)]
    for color in range(NCOLOR):
        for i in range(per_group):
            stacked = jnp.concatenate(
                [tiles[g * per_group + i, pl.ds(color, COLS, stride=NCOLOR), :] for g in range(GROUPS)], axis=0
            )
            turned[pl.ds(128 * i, 128), :] = stacked.T
        for partner, out_ref in zip(partners, out_refs):
            r = jnp.bitwise_xor(index_ref[0], partner)
            out_ref[pl.ds(color * rows, rows), :] = turned[pl.ds(r, rows, stride=count), :]


def split_kernel(vec_ref, high_ref, low_ref, landed, arrived):
    width = vec_ref.shape[3] // GROUPS
    steps = [(part, color) for color in range(NCOLOR) for part in range(2)]
    copies = [
        pltpu.make_async_copy(vec_ref.at[part, color], landed.at[part, color], arrived.at[i])
        for i, (part, color) in enumerate(steps)
    ]
    for copy in copies:
        copy.start()
    for color in range(NCOLOR):
        for copy in copies[2 * color : 2 * color + 2]:
            copy.wait()
        for g in range(GROUPS):
            rows = pl.ds((g * NCOLOR + color) * width, width)
            both = jnp.concatenate([landed[part, color, :, pl.ds(g * width, width)] for part in range(2)], axis=0)
            high, low = split(both.T)
            high_ref[rows, :] = high
            low_ref[rows, :] = low


def project_kernel(partners, index_ref, *refs):
    count = len(partners)
    field_refs = refs[:count]
    high_ref, low_ref, noise_ref, block_ref, sums_ref, line_ref, weights = refs[count:]
    width = high_ref.shape[0] // (GROUPS * NCOLOR)
    rows = width // count
    for partner, field_ref in zip(partners, field_refs):
        s = jnp.bitwise_xor(index_ref[0], partner)
        for color in range(NCOLOR):
            weights[pl.ds(color * width + s, rows, stride=count), :] = field_ref[pl.ds(color * rows, rows), :]
    high, low = split(weights[...].T)
    dims = (((1,), (1,)), ((), ()))
    total = jnp.zeros((COLS, 2 * NEIG), jnp.float32)
    for g in range(GROUPS):
        vecs, columns = pl.ds(g * NCOLOR * width, NCOLOR * width), slice(g * COLS, (g + 1) * COLS)
        both = jnp.concatenate([high[columns], low[columns]], axis=0)
        first = jnp.dot(both, high_ref[vecs, :], preferred_element_type=jnp.float32)
        second = jnp.dot(high[columns], low_ref[vecs, :], preferred_element_type=jnp.float32)
        total += first[:COLS] + (first[COLS:] + second)
    with_real, with_imag = total[:, :NEIG], total[:, NEIG:]
    real = with_real[:PAIRS] + with_imag[PAIRS:]
    imag = with_real[PAIRS:] - with_imag[:PAIRS]
    noise = jnp.concatenate(
        [jnp.broadcast_to(noise_ref[pl.ds(spin, 1), :], (NSPIN, NEIG)) for spin in range(NSPIN)], axis=0
    )
    zreal = (noise == 0).astype(jnp.float32) - (noise == 2).astype(jnp.float32)
    zimag = (noise == 1).astype(jnp.float32) - (noise == 3).astype(jnp.float32)
    line = jnp.concatenate([zreal * real + zimag * imag, zreal * imag - zimag * real], axis=0)
    blocks = lax.broadcasted_iota(jnp.int32, (NBLOCK, NEIG), 0)
    onehot = (blocks == block_ref[...]).astype(jnp.bfloat16)
    line_high, line_low = split(line)
    line_sum = lax.dot_general(onehot, line_high, dims, preferred_element_type=jnp.float32)
    line_sum += lax.dot_general(onehot, line_low, dims, preferred_element_type=jnp.float32)
    sums_ref[...] = jnp.concatenate([real, imag], axis=0)
    line_ref[...] = jnp.concatenate([jnp.zeros((8, LINE_LANE), jnp.float32), line_sum], axis=1)


def spread_kernel(sums_ref, line_ref, out_ref):
    count = out_ref.shape[0]
    per = NEIG // count
    sums = sums_ref[...]
    for j in range(count):
        pieces = [sums[8 * i : 8 * i + 8, per * j : per * (j + 1)] for i in range(COLS // 8)]
        pieces.append(jnp.zeros((8, 128 - per * len(pieces)), jnp.float32))
        out_ref[j] = jnp.concatenate(pieces, axis=1) + line_ref[...]


def join_kernel(part_ref, line_ref, out_ref):
    count = part_ref.shape[0]
    for j in range(count):
        part = part_ref[j] + line_ref[...]
        for i in range(out_ref.shape[0]):
            out_ref[i, count - 1 - j] = part


def finish_kernel(count, factor, index_ref, parts_ref, rows_ref, line_ref):
    per = NEIG // count
    own = jnp.sum(parts_ref[parts_ref.shape[0] - 1 - index_ref[0] // CORES], axis=0)
    for i in range(COLS // 8):
        rows_ref[pl.ds(8 * i, 8), :] = own[:, per * i : per * (i + 1)]
    whole = jnp.sum(jnp.sum(parts_ref[...], axis=1), axis=0)
    turned = whole.T[LINE_LANE:]
    for part in range(2):
        first = PAIRS * part
        line_ref[part] = factor * sum(turned[first + NSPIN * s : first + NSPIN * (s + 1)] for s in range(NSPIN))


def body(solutions, eigvecs, sink_noise, eig_block):
    count = lax.axis_size("slab")
    times = lax.axis_size("tm")
    sites = solutions.shape[-1]
    rows = NCOLOR * sites // GROUPS // count
    per = NEIG // count
    f32 = jnp.float32
    index = lax.axis_index("slab").reshape(1)
    time = lax.axis_index("tm").reshape(1)
    far = [p for p in ORDER if p < count]
    partners = [0] + far + [p for p in range(1, count) if p not in far]
    chunks = pl.pallas_call(
        functools.partial(pack_kernel, partners),
        out_shape=[jax.ShapeDtypeStruct((rows, 128), f32)] * count,
        in_specs=[SMEM, SMEM, VMEM],
        out_specs=[VMEM] * count,
        scratch_shapes=[pltpu.VMEM((sites // 128, NCOLOR * COLS, 128), f32), pltpu.VMEM((sites // GROUPS, 128), f32)],
        compiler_params=pltpu.CompilerParams(vmem_limit_bytes=8 * 1024 * 1024),
        name="pack",
    )(index, time, solutions.reshape(solutions.shape[1:]))
    received = [
        lax.ppermute(chunk, "slab", [(i, i ^ partner) for i in range(count)]) if partner else chunk
        for partner, chunk in zip(partners, chunks)
    ]
    vectors = jnp.transpose(eigvecs.reshape(eigvecs.shape[1:]), (0, 2, 1, 3))
    shape = jax.ShapeDtypeStruct((NCOLOR * sites, 2 * NEIG), jnp.bfloat16)
    high, low = pl.pallas_call(
        split_kernel,
        out_shape=(shape, shape),
        in_specs=[pl.BlockSpec(memory_space=pltpu.HBM)],
        out_specs=(VMEM, VMEM),
        scratch_shapes=[pltpu.VMEM(vectors.shape, f32), pltpu.SemaphoreType.DMA((2 * NCOLOR,))],
        compiler_params=pltpu.CompilerParams(vmem_limit_bytes=24 * 1024 * 1024),
        cost_estimate=pl.CostEstimate(flops=6 * eigvecs.size, bytes_accessed=8 * eigvecs.size, transcendentals=0),
        name="split",
    )(pltpu.with_memory_space_constraint(vectors, pltpu.HBM))
    sums, line = pl.pallas_call(
        functools.partial(project_kernel, partners),
        out_shape=(pltpu.VMEM((COLS, NEIG), f32), pltpu.VMEM((8, 128), f32)),
        in_specs=[SMEM] + [VMEM] * (count + 4),
        out_specs=(VMEM, VMEM),
        scratch_shapes=[pltpu.VMEM((NCOLOR * sites // GROUPS, 128), f32)],
        compiler_params=pltpu.CompilerParams(vmem_limit_bytes=24 * 1024 * 1024),
        name="project",
    )(index, *received, high, low, jnp.transpose(sink_noise.reshape(NEIG, NSPIN)), eig_block.reshape(1, NEIG))
    other_line = lax.ppermute(line, "tm", [(i, i ^ 1) for i in range(times)])
    part = pl.pallas_call(
        spread_kernel,
        out_shape=pltpu.VMEM((count, 8, 128), f32),
        in_specs=[VMEM, VMEM],
        out_specs=VMEM,
        compiler_params=pltpu.CompilerParams(vmem_limit_bytes=8 * 1024 * 1024),
        name="spread",
    )(sums, line)
    chips = times // CORES
    parts = pl.pallas_call(
        join_kernel,
        out_shape=pltpu.VMEM((chips, count, 8, 128), f32),
        in_specs=[VMEM, VMEM],
        out_specs=VMEM,
        compiler_params=pltpu.CompilerParams(vmem_limit_bytes=8 * 1024 * 1024),
        name="join",
    )(part, other_line)
    groups = [
        [(chip * CORES + core) * count + s for chip in reversed(range(chips)) for s in reversed(range(count))]
        for core in range(CORES)
    ]
    parts = lax.all_to_all(
        parts.reshape(chips * count, 8, 128), ("tm", "slab"), 0, 0, axis_index_groups=groups, tiled=True
    )
    factor = 1.0 / math.sqrt(times * NEIG * NSPIN / NBLOCK)
    own_rows, line = pl.pallas_call(
        functools.partial(finish_kernel, count, factor),
        out_shape=(jax.ShapeDtypeStruct((COLS, per), f32), jax.ShapeDtypeStruct((2, NSPIN, NBLOCK), f32)),
        in_specs=[SMEM, VMEM],
        out_specs=(VMEM, VMEM),
        compiler_params=pltpu.CompilerParams(vmem_limit_bytes=8 * 1024 * 1024),
        name="finish",
    )(time, parts.reshape(chips, count, 8, 128))
    projected = jnp.transpose(own_rows).reshape(per, 1, 2, PAIRS)
    return projected, jnp.transpose(line, (0, 2, 1))


def solution(mesh):
    in_specs = (P("tm", None, "slab"), P("tm", None, None, None, "slab"), P(None, "tm", None), P())
    out_specs = (P("slab", "tm", None, None), P())
    return jax.shard_map(body, mesh=mesh, in_specs=in_specs, out_specs=out_specs, check_vma=False)
```

```python
import functools
import math

import jax
import jax.numpy as jnp
from jax import lax
from jax.experimental import pallas as pl
from jax.experimental.pallas import tpu as pltpu
from jax.sharding import PartitionSpec as P

NSPIN = 4
NCOLOR = 3
NEIG = 192
NBLOCK = 8
PAIRS = NSPIN * NSPIN
COLS = 2 * PAIRS
GROUPS = 128 // COLS
CORES = 2
EARLY = 3
LINE_LANE = 96

ORDER = (4, 3, 6, 5, 7, 2, 1)

VMEM = pl.BlockSpec(memory_space=pltpu.VMEM)
SMEM = pl.BlockSpec(memory_space=pltpu.SMEM)


def split(value):
    high = value.astype(jnp.bfloat16)
    low = (value - high.astype(jnp.float32)).astype(jnp.bfloat16)
    return high, low


def pack_kernel(partners, index_ref, time_ref, sol_ref, *refs):
    out_refs, (tiles, turned) = refs[: len(partners)], refs[len(partners) :]
    count = len(partners)
    width = sol_ref.shape[1] // GROUPS
    rows = width // count
    per_group = width // 128
    for i in range(tiles.shape[0]):
        tiles[i] = sol_ref[:, pl.ds(128 * i, 128)]
    for color in range(NCOLOR):
        for i in range(per_group):
            stacked = jnp.concatenate(
                [tiles[g * per_group + i, pl.ds(color, COLS, stride=NCOLOR), :] for g in range(GROUPS)], axis=0
            )
            turned[pl.ds(128 * i, 128), :] = stacked.T
        for partner, out_ref in zip(partners, out_refs):
            r = jnp.bitwise_xor(index_ref[0], partner)
            out_ref[pl.ds(color * rows, rows), :] = turned[pl.ds(r, rows, stride=count), :]


def place(count, partners, index_ref, field_refs, weights):
    rows = weights.shape[0] // count
    for partner, field_ref in zip(partners, field_refs):
        s = jnp.bitwise_xor(index_ref[0], partner)
        weights[pl.ds(s, rows, stride=count), :] = field_ref[...]


def split_kernel(count, partners, index_ref, *refs):
    field_refs = refs[: len(partners)]
    vec_ref, high_ref, low_ref, weights, landed, arrived = refs[len(partners) :]
    width = vec_ref.shape[3] // GROUPS
    steps = [(part, color) for color in range(NCOLOR) for part in range(2)]
    copies = [
        pltpu.make_async_copy(vec_ref.at[part, color], landed.at[part, color], arrived.at[i])
        for i, (part, color) in enumerate(steps)
    ]
    for copy in copies:
        copy.start()
    place(count, partners, index_ref, field_refs, weights)
    for color in range(NCOLOR):
        for copy in copies[2 * color : 2 * color + 2]:
            copy.wait()
        for g in range(GROUPS):
            rows = pl.ds((g * NCOLOR + color) * width, width)
            both = jnp.concatenate([landed[part, color, :, pl.ds(g * width, width)] for part in range(2)], axis=0)
            high, low = split(both.T)
            high_ref[rows, :] = high
            low_ref[rows, :] = low


def project_kernel(count, partners, index_ref, *refs):
    field_refs = refs[: len(partners)]
    _, high_ref, low_ref, noise_ref, block_ref, sums_ref, line_ref, weights = refs[len(partners) :]
    width = high_ref.shape[0] // (GROUPS * NCOLOR)
    place(count, partners, index_ref, field_refs, weights)
    high, low = split(weights[...].T)
    dims = (((1,), (1,)), ((), ()))
    total = jnp.zeros((COLS, 2 * NEIG), jnp.float32)
    for g in range(GROUPS):
        vecs, columns = pl.ds(g * NCOLOR * width, NCOLOR * width), slice(g * COLS, (g + 1) * COLS)
        both = jnp.concatenate([high[columns], low[columns]], axis=0)
        first = jnp.dot(both, high_ref[vecs, :], preferred_element_type=jnp.float32)
        second = jnp.dot(high[columns], low_ref[vecs, :], preferred_element_type=jnp.float32)
        total += first[:COLS] + (first[COLS:] + second)
    with_real, with_imag = total[:, :NEIG], total[:, NEIG:]
    real = with_real[:PAIRS] + with_imag[PAIRS:]
    imag = with_real[PAIRS:] - with_imag[:PAIRS]
    noise = jnp.concatenate(
        [jnp.broadcast_to(noise_ref[pl.ds(spin, 1), :], (NSPIN, NEIG)) for spin in range(NSPIN)], axis=0
    )
    zreal = (noise == 0).astype(jnp.float32) - (noise == 2).astype(jnp.float32)
    zimag = (noise == 1).astype(jnp.float32) - (noise == 3).astype(jnp.float32)
    line = jnp.concatenate([zreal * real + zimag * imag, zreal * imag - zimag * real], axis=0)
    blocks = lax.broadcasted_iota(jnp.int32, (NBLOCK, NEIG), 0)
    onehot = (blocks == block_ref[...]).astype(jnp.bfloat16)
    line_high, line_low = split(line)
    line_sum = lax.dot_general(onehot, line_high, dims, preferred_element_type=jnp.float32)
    line_sum += lax.dot_general(onehot, line_low, dims, preferred_element_type=jnp.float32)
    sums_ref[...] = jnp.concatenate([real, imag], axis=0)
    line_ref[...] = jnp.concatenate([jnp.zeros((8, LINE_LANE), jnp.float32), line_sum], axis=1)


def spread_kernel(sums_ref, line_ref, out_ref):
    count = out_ref.shape[0]
    per = NEIG // count
    sums = sums_ref[...]
    for j in range(count):
        pieces = [sums[8 * i : 8 * i + 8, per * j : per * (j + 1)] for i in range(COLS // 8)]
        pieces.append(jnp.zeros((8, 128 - per * len(pieces)), jnp.float32))
        out_ref[j] = jnp.concatenate(pieces, axis=1) + line_ref[...]


def join_kernel(part_ref, line_ref, out_ref):
    count = part_ref.shape[0]
    for j in range(count):
        part = part_ref[j] + line_ref[...]
        for i in range(out_ref.shape[0]):
            out_ref[i, count - 1 - j] = part


def finish_kernel(count, factor, index_ref, parts_ref, rows_ref, line_ref):
    per = NEIG // count
    own = jnp.sum(parts_ref[parts_ref.shape[0] - 1 - index_ref[0] // CORES], axis=0)
    for i in range(COLS // 8):
        rows_ref[pl.ds(8 * i, 8), :] = own[:, per * i : per * (i + 1)]
    whole = jnp.sum(jnp.sum(parts_ref[...], axis=1), axis=0)
    turned = whole.T[LINE_LANE:]
    for part in range(2):
        first = PAIRS * part
        line_ref[part] = factor * sum(turned[first + NSPIN * s : first + NSPIN * (s + 1)] for s in range(NSPIN))


def body(solutions, eigvecs, sink_noise, eig_block):
    count = lax.axis_size("slab")
    times = lax.axis_size("tm")
    sites = solutions.shape[-1]
    rows = NCOLOR * sites // GROUPS // count
    per = NEIG // count
    f32 = jnp.float32
    index = lax.axis_index("slab").reshape(1)
    time = lax.axis_index("tm").reshape(1)
    far = [p for p in ORDER if p < count]
    partners = [0] + far + [p for p in range(1, count) if p not in far]
    chunks = pl.pallas_call(
        functools.partial(pack_kernel, partners),
        out_shape=[jax.ShapeDtypeStruct((rows, 128), f32)] * count,
        in_specs=[SMEM, SMEM, VMEM],
        out_specs=[VMEM] * count,
        scratch_shapes=[pltpu.VMEM((sites // 128, NCOLOR * COLS, 128), f32), pltpu.VMEM((sites // GROUPS, 128), f32)],
        compiler_params=pltpu.CompilerParams(vmem_limit_bytes=8 * 1024 * 1024),
        name="pack",
    )(index, time, solutions.reshape(solutions.shape[1:]))
    received = [
        lax.ppermute(chunk, "slab", [(i, i ^ partner) for i in range(count)]) if partner else chunk
        for partner, chunk in zip(partners, chunks)
    ]
    vectors = jnp.transpose(eigvecs.reshape(eigvecs.shape[1:]), (0, 2, 1, 3))
    shape = jax.ShapeDtypeStruct((NCOLOR * sites, 2 * NEIG), jnp.bfloat16)
    field = pltpu.VMEM((NCOLOR * sites // GROUPS, 128), f32)
    high, low, placed = pl.pallas_call(
        functools.partial(split_kernel, count, partners[:EARLY]),
        out_shape=(shape, shape, field),
        in_specs=[SMEM] + [VMEM] * EARLY + [pl.BlockSpec(memory_space=pltpu.HBM)],
        out_specs=(VMEM, VMEM, VMEM),
        scratch_shapes=[pltpu.VMEM(vectors.shape, f32), pltpu.SemaphoreType.DMA((2 * NCOLOR,))],
        compiler_params=pltpu.CompilerParams(vmem_limit_bytes=24 * 1024 * 1024),
        cost_estimate=pl.CostEstimate(flops=6 * eigvecs.size, bytes_accessed=8 * eigvecs.size, transcendentals=0),
        name="split",
    )(index, *received[:EARLY], pltpu.with_memory_space_constraint(vectors, pltpu.HBM))
    sums, line, _ = pl.pallas_call(
        functools.partial(project_kernel, count, partners[EARLY:]),
        out_shape=(pltpu.VMEM((COLS, NEIG), f32), pltpu.VMEM((8, 128), f32), field),
        in_specs=[SMEM] + [VMEM] * (count - EARLY + 5),
        out_specs=(VMEM, VMEM, VMEM),
        input_output_aliases={count - EARLY + 1: 2},
        compiler_params=pltpu.CompilerParams(vmem_limit_bytes=24 * 1024 * 1024),
        name="project",
    )(
        index,
        *received[EARLY:],
        placed,
        high,
        low,
        jnp.transpose(sink_noise.reshape(NEIG, NSPIN)),
        eig_block.reshape(1, NEIG),
    )
    other_line = lax.ppermute(line, "tm", [(i, i ^ 1) for i in range(times)])
    part = pl.pallas_call(
        spread_kernel,
        out_shape=pltpu.VMEM((count, 8, 128), f32),
        in_specs=[VMEM, VMEM],
        out_specs=VMEM,
        compiler_params=pltpu.CompilerParams(vmem_limit_bytes=8 * 1024 * 1024),
        name="spread",
    )(sums, line)
    chips = times // CORES
    parts = pl.pallas_call(
        join_kernel,
        out_shape=pltpu.VMEM((chips, count, 8, 128), f32),
        in_specs=[VMEM, VMEM],
        out_specs=VMEM,
        compiler_params=pltpu.CompilerParams(vmem_limit_bytes=8 * 1024 * 1024),
        name="join",
    )(part, other_line)
    groups = [
        [(chip * CORES + core) * count + s for chip in reversed(range(chips)) for s in reversed(range(count))]
        for core in range(CORES)
    ]
    parts = lax.all_to_all(
        parts.reshape(chips * count, 8, 128), ("tm", "slab"), 0, 0, axis_index_groups=groups, tiled=True
    )
    factor = 1.0 / math.sqrt(times * NEIG * NSPIN / NBLOCK)
    own_rows, line = pl.pallas_call(
        functools.partial(finish_kernel, count, factor),
        out_shape=(jax.ShapeDtypeStruct((COLS, per), f32), jax.ShapeDtypeStruct((2, NSPIN, NBLOCK), f32)),
        in_specs=[SMEM, VMEM],
        out_specs=(VMEM, VMEM),
        compiler_params=pltpu.CompilerParams(vmem_limit_bytes=8 * 1024 * 1024),
        name="finish",
    )(time, parts.reshape(chips, count, 8, 128))
    projected = jnp.transpose(own_rows).reshape(per, 1, 2, PAIRS)
    return projected, jnp.transpose(line, (0, 2, 1))


def solution(mesh):
    in_specs = (P("tm", None, "slab"), P("tm", None, None, None, "slab"), P(None, "tm", None), P())
    out_specs = (P("slab", "tm", None, None), P())
    return jax.shard_map(body, mesh=mesh, in_specs=in_specs, out_specs=out_specs, check_vma=False)
```
